256 devices in a mesh: row: 32 (over z_hi, y, core), col: 8 (over z_lo, x).
Axes of the slice: x: 4, y: 4, z: 8 (z_hi: 4, z_lo: 2; z = z_hi * 2 + z_lo), core: 2. Of those that a mesh axis runs over, the one named last changes fastest.
Arguments:
- clips: bfloat16 [20480, 1024], P(('row', 'col')), may hold values from -8 to 8
- labels: int32 [20480], P(('row', 'col')), may hold values from 0 to 1023
Outputs:
- distances: float32 [20480, 1024], P(('row', 'col'))
The draws below stay inside these ranges and needn't reach their ends.
All inputs are finite; a program needn't handle non-finite values.
Results may differ from the reference program's by a relative error of at most 0.002.
Values may be sent and summed in bfloat16 or wider, within the bound.
No kernel may reach another device: no remote copies, remote signals or barrier semaphores. Data moves between devices by JAX's collectives and lax.ppermute only.
A program may use at most 64 MiB of HBM per device.

```python
import math
import jax
import jax.numpy as jnp
import numpy as np
from jax import lax

D = 1024
CLUSTERS = 1024
ROWS_DEV = 80
CLIPS = 20480


def draw_clips(key, part):
    key = jax.random.fold_in(key, 5)
    scale_key, group_key, centre_key, noise_key = jax.random.split(key, 4)
    group_count = 48
    groups = jax.random.randint(group_key, (CLIPS,), 0, group_count)
    scales = jnp.exp(jax.random.uniform(scale_key, (CLIPS, 1), jnp.float32, jnp.log(0.6), jnp.log(1.6)))
    centres = jax.random.normal(centre_key, (group_count, D), jnp.float32)
    noise = jax.random.normal(noise_key, (CLIPS, D), jnp.float32)
    values = (jnp.take(centres, groups, axis=0) + noise) * scales
    return jnp.clip(values, -8.0, 8.0).astype(jnp.bfloat16)


def plant(array, key, least, top_value):
    longest = array.shape.index(max(array.shape))
    spots = []
    for shift in (0, 1):
        where = [jax.random.randint(jax.random.fold_in(key, axis), (), 0, length) for axis, length in enumerate(array.shape)]
        where[longest] = (where[longest] + shift) % array.shape[longest]
        spots.append(tuple(where))
    return array.at[spots[0]].set(least).at[spots[1]].set(top_value)


def rank_bounds(number_of, skew):
    portions = [(1 << 20) // math.isqrt(rank ** skew) + 1 for rank in range(1, number_of + 1)]
    deviation = 1 + sum(portions) // (1 << 30)
    return np.cumsum(np.array([max(1, weight // deviation) for weight in portions]))


def ranked_ids(stream_key, extent, count, skew):
    table = rank_bounds(count, skew)
    pick = jax.random.randint(jax.random.fold_in(stream_key, 1), extent, 0, int(table[count - 1]))
    standing = jnp.searchsorted(jnp.asarray(table, jnp.int32), pick, side="right")
    return jax.random.permutation(jax.random.fold_in(stream_key, 2), count)[standing].astype(jnp.int32)


def setup_inputs(seed: int = 0) -> dict:
    arg_keys = jax.random.split(jax.random.key(seed), 3)
    clips = draw_clips(jax.random.fold_in(arg_keys[2], 71), 0)
    labels = plant(ranked_ids(arg_keys[1], (CLIPS,), CLUSTERS, 2), jax.random.fold_in(arg_keys[1], 3), 0, CLUSTERS - 1).astype(jnp.int32)
    return {"clips": clips, "labels": labels}


def reference(clips, labels):
    wide = clips.astype(jnp.float32)
    norms = jnp.sum(wide * wide, axis=1)
    shards = CLIPS // ROWS_DEV
    blocks = clips.reshape(shards, ROWS_DEV, D)
    block_norms = norms.reshape(shards, ROWS_DEV)

    def one_block(packed):
        rows_block, rows_norms = packed
        inner = lax.dot_general(rows_block, clips, (((1,), (1,)), ((), ())), preferred_element_type=jnp.float32)
        dist_sq = rows_norms[:, None] + norms[None, :] - 2.0 * inner
        kernel = jnp.exp(-dist_sq * (0.5 / D))
        summed = jax.ops.segment_sum(kernel.T, labels, num_segments=CLUSTERS)
        return summed.T

    similar = lax.map(one_block, (blocks, block_norms)).reshape(CLIPS, CLUSTERS)
    counts = jax.ops.segment_sum(jnp.ones((CLIPS,), jnp.float32), labels, num_segments=CLUSTERS)
    own_terms = jnp.take_along_axis(similar, labels[:, None].astype(jnp.int32), axis=1)[:, 0]
    totals = jax.ops.segment_sum(own_terms, labels, num_segments=CLUSTERS)
    sizes = jnp.maximum(counts, 1.0)
    return 1.0 - 2.0 * similar / sizes[None, :] + (totals / (sizes * sizes))[None, :]
```

```python
import functools

import jax
import jax.numpy as jnp
from jax import lax
from jax.experimental import pallas as pl
from jax.experimental.pallas import tpu as pltpu
from jax.sharding import Mesh, PartitionSpec as P

D = 1024
CLUSTERS = 1024
META = 128
WIDE = D + META
ROWS = 80
LOG2E = 1.4426950408889634
SCALE = LOG2E / D
F32 = jnp.float32
BF16 = jnp.bfloat16
TRANSPOSED = (((1,), (1,)), ((), ()))
AXES = ("z_hi", "y", "core", "z_lo", "x")
SIZES = (4, 4, 2, 2, 4)
Z = ("z_hi", "z_lo")
PLANE = ("y", "core", "x")


def call(body, outs, cost, *args):
    flops, size = cost
    return pl.pallas_call(
        body,
        out_shape=outs,
        compiler_params=pltpu.CompilerParams(vmem_limit_bytes=40 * 2**20),
        cost_estimate=pl.CostEstimate(flops=flops, bytes_accessed=size, transcendentals=0),
    )(*args)


def shape(dims, dtype):
    return jax.ShapeDtypeStruct(dims, dtype)


def pack_kernel(clips_ref, labels_ref, out_ref):
    x = clips_ref[...]
    wide = x.astype(F32)
    half = jnp.sum(wide * wide, axis=1, keepdims=True) * (0.5 * SCALE)
    row = lax.broadcasted_iota(jnp.int32, (ROWS, ROWS), 0)
    col = lax.broadcasted_iota(jnp.int32, (ROWS, ROWS), 1)
    same = row == col
    label = jnp.sum(jnp.where(same, labels_ref[...].astype(F32), 0.0), axis=1, keepdims=True)
    half_row = jnp.sum(jnp.where(same, half, 0.0), axis=0, keepdims=True)
    gram = lax.dot_general(x, x, TRANSPOSED, preferred_element_type=F32)
    near = jnp.exp2(gram * SCALE - half - half_row)
    offset = jnp.sum(jnp.where(same, 0.0, near), axis=1, keepdims=True) * (1.0 / (ROWS - 1))
    first = half.astype(BF16).astype(F32)
    second = (half - first).astype(BF16).astype(F32)
    third = half - first - second
    upper = jnp.floor(label * (1.0 / 32.0))
    lower = label - 32.0 * upper
    lane = lax.broadcasted_iota(jnp.int32, (ROWS, META), 1)
    meta = jnp.zeros((ROWS, META), F32)
    for place, value in enumerate((first, second, third, upper, lower, offset)):
        meta = jnp.where(lane == place, value, meta)
    out_ref[:, :D] = x
    out_ref[:, D:] = meta.astype(BF16)


def split_meta(meta):
    wide = meta.astype(F32)
    half = wide[:, 0:1] + wide[:, 1:2] + wide[:, 2:3]
    label = (wide[:, 3:4] * 32.0 + wide[:, 4:5]).astype(jnp.int32)
    return half, label, wide[:, 5:6]


def prep_kernel(block_ref, member_ref, half_ref, count_ref):
    rows = block_ref.shape[0]
    meta = block_ref[:, D:]
    lane = lax.broadcasted_iota(jnp.int32, (8, META), 1)
    pick = jnp.where(lane < 3, 1.0, 0.0).astype(BF16)
    half_ref[...] = lax.dot_general(pick, meta, TRANSPOSED, preferred_element_type=F32)
    _, label, _ = split_meta(meta)
    ids = lax.broadcasted_iota(jnp.int32, (rows, CLUSTERS), 1)
    member = jnp.where(label == ids, 1.0, 0.0)
    count_ref[...] = jnp.sum(member.reshape(rows // 8, 8, CLUSTERS), axis=0)
    member_ref[...] = member.astype(BF16)


def prep(block):
    rows = block.shape[0]
    outs = (
        shape((rows, CLUSTERS), BF16),
        shape((8, rows), F32),
        shape((8, CLUSTERS), F32),
    )
    return call(prep_kernel, outs, (rows * CLUSTERS * 4, rows * 4096), block)


def main_kernel(pieces, blocks, *refs):
    piece_refs, refs = refs[:pieces], refs[pieces:]
    block_refs, refs = refs[:blocks], refs[blocks:]
    member_refs, refs = refs[:blocks], refs[blocks:]
    half_refs, refs = refs[:blocks], refs[blocks:]
    count_refs, refs = refs[:blocks], refs[blocks:]
    out_refs, total_ref = refs[:pieces], refs[pieces]
    rows = jnp.concatenate([ref[...] for ref in piece_refs], axis=0)
    left = rows[:, :D]
    half, label, offset = split_meta(rows[:, D:])
    sums = None
    count = None
    for block, member, half_row, one_count in zip(block_refs, member_refs, half_refs, count_refs):
        gram = lax.dot_general(left, block[:, :D], TRANSPOSED, preferred_element_type=F32)
        kernel = jnp.exp2(gram * SCALE - half - half_row[0:1, :]) - offset
        term = jnp.dot(kernel.astype(BF16), member[...], preferred_element_type=F32)
        sums = term if sums is None else sums + term
        count = one_count[...] if count is None else count + one_count[...]
    count = jnp.sum(count, axis=0, keepdims=True)
    ids = lax.broadcasted_iota(jnp.int32, sums.shape, 1)
    own = jnp.where(label == ids, sums + offset * count, 0.0)
    total_ref[...] = jnp.sum(own.reshape(own.shape[0] // 8, 8, CLUSTERS), axis=0)
    for place, ref in enumerate(out_refs):
        ref[...] = sums[place * ROWS : (place + 1) * ROWS].astype(ref.dtype)


def main(pieces, types, blocks, members, halves, counts):
    outs = tuple(shape((ROWS, CLUSTERS), dtype) for dtype in types) + (shape((8, CLUSTERS), F32),)
    flops = 4 * ROWS * len(pieces) * 2560 * 1024
    size = sum(a.size * 2 for a in (*pieces, *blocks, *members))
    return call(
        functools.partial(main_kernel, len(pieces), len(blocks)),
        outs, (flops, size), *pieces, *blocks, *members, *halves, *counts,
    )


def sums_kernel(count, *refs):
    values = [ref[...] for ref in refs[: count * 2]]
    total = functools.reduce(jnp.add, values[:count])
    number = functools.reduce(jnp.add, values[count:])
    out_ref = refs[-1]
    out_ref[...] = jnp.concatenate(
        [
            jnp.sum(total, axis=0, keepdims=True),
            jnp.sum(number, axis=0, keepdims=True) * (1.0 / 32.0),
            jnp.zeros((6, CLUSTERS), F32),
        ],
        axis=0,
    )


def final_kernel(own_ref, packed_ref, sums_ref, *refs):
    out_ref = refs[-1]
    similar = own_ref[...]
    for ref in refs[:-1]:
        similar = similar + ref[...].astype(F32)
    _, _, offset = split_meta(packed_ref[:, D:])
    totals = sums_ref[0:1, :]
    counts = sums_ref[1:2, :]
    sizes = jnp.maximum(counts, 1.0)
    inverse = 1.0 / sizes
    similar = similar + offset * counts
    out_ref[...] = 1.0 - 2.0 * (similar * inverse) + totals * inverse * inverse


def local(clips, labels):
    def shift(value, axis, step):
        names = axis if isinstance(axis, tuple) else (axis,)
        size = 1
        for name in names:
            size *= SIZES[AXES.index(name)]
        return lax.ppermute(value, axis, [(i, (i + step) % size) for i in range(size)])

    def plane_shift(value, stage, step):
        pairs = []
        for y in range(4):
            for core in range(2):
                for x in range(4):
                    if (core == 0) == (stage == 1):
                        to_y, to_x = y, (x + step) % 4
                    else:
                        to_y, to_x = (y + step) % 4, x
                    pairs.append(((y * 2 + core) * 4 + x, (to_y * 2 + core) * 4 + to_x))
        return lax.ppermute(value, PLANE, pairs)

    own = call(
        pack_kernel, shape((ROWS, WIDE), BF16), (10**6, ROWS * WIDE * 4),
        clips, labels.reshape(1, ROWS),
    )
    near = [plane_shift(own, 1, step) for step in (1, -1, 2)]
    up, down = [own], [own]
    up.append(shift(own, Z, 1))
    down.append(shift(own, Z, -1))
    four = jnp.concatenate([own, *near], axis=0)
    blocks = [four] + [plane_shift(four, 2, step) for step in (1, -1, 2)]
    blocks += [shift(block, "core", 1) for block in blocks]
    for _ in range(2):
        up.append(shift(up[-1], Z, 1))
        down.append(shift(down[-1], Z, -1))
    up.append(shift(up[-1], Z, 1))
    prepared = [prep(block) for block in blocks]
    members, halves, counts = zip(*prepared)

    received, totals = [], []
    for step in (1, 2, 3):
        first, second, total = main(
            (up[step], down[step]), (BF16, BF16), blocks, members, halves, counts
        )
        received += [shift(first, Z, -step), shift(second, Z, step)]
        totals.append(total)
    far, similar, total = main((up[4], own), (BF16, F32), blocks, members, halves, counts)
    received.append(shift(far, Z, -4))
    totals.append(total)
    totals += [jnp.zeros((8, CLUSTERS), F32)] * 4
    sums = call(
        functools.partial(sums_kernel, 8), shape((8, CLUSTERS), F32), (10**5, 10**6),
        *totals, *counts,
    )
    for axis in ("x", "y"):
        parts = [shift(sums, axis, step) for step in (1, 2, 3)]
        sums = sums + parts[0] + parts[1] + parts[2]
    sums = sums + shift(sums, "core", 1)
    parts = [shift(sums, Z, step) for step in range(1, 8)]
    sums = functools.reduce(jnp.add, parts, sums)
    return call(
        final_kernel, shape((ROWS, CLUSTERS), F32), (10**6, 2 * 10**6),
        similar, own, sums, *received,
    )


def solution(mesh):
    fine = Mesh(mesh.devices.reshape(SIZES), AXES)
    return jax.shard_map(
        local, mesh=fine, in_specs=(P(AXES, None), P(AXES)), out_specs=P(AXES, None), check_vma=False
    )
```

```python
import functools

import jax
import jax.numpy as jnp
from jax import lax
from jax.experimental import pallas as pl
from jax.experimental.pallas import tpu as pltpu
from jax.sharding import Mesh, PartitionSpec as P

D = 1024
CLUSTERS = 1024
META = 128
WIDE = D + META
ROWS = 80
LOG2E = 1.4426950408889634
SCALE = LOG2E / D
F32 = jnp.float32
BF16 = jnp.bfloat16
TRANSPOSED = (((1,), (1,)), ((), ()))
AXES = ("z_hi", "y", "core", "z_lo", "x")
SIZES = (4, 4, 2, 2, 4)
Z = ("z_hi", "z_lo")
PLANE = ("y", "core", "x")


def call(body, outs, cost, *args):
    flops, size = 0, 0
    return pl.pallas_call(
        body,
        out_shape=outs,
        compiler_params=pltpu.CompilerParams(vmem_limit_bytes=40 * 2**20),
        cost_estimate=pl.CostEstimate(flops=flops, bytes_accessed=size, transcendentals=0),
    )(*args)


def shape(dims, dtype):
    return jax.ShapeDtypeStruct(dims, dtype)


def pack_kernel(clips_ref, labels_ref, out_ref):
    x = clips_ref[...]
    wide = x.astype(F32)
    half = jnp.sum(wide * wide, axis=1, keepdims=True) * (0.5 * SCALE)
    row = lax.broadcasted_iota(jnp.int32, (ROWS, ROWS), 0)
    col = lax.broadcasted_iota(jnp.int32, (ROWS, ROWS), 1)
    same = row == col
    label = jnp.sum(jnp.where(same, labels_ref[...].astype(F32), 0.0), axis=1, keepdims=True)
    half_row = jnp.sum(jnp.where(same, half, 0.0), axis=0, keepdims=True)
    gram = lax.dot_general(x, x, TRANSPOSED, preferred_element_type=F32)
    near = jnp.exp2(gram * SCALE - half - half_row)
    offset = jnp.sum(jnp.where(same, 0.0, near), axis=1, keepdims=True) * (1.0 / (ROWS - 1))
    first = half.astype(BF16).astype(F32)
    second = (half - first).astype(BF16).astype(F32)
    third = half - first - second
    upper = jnp.floor(label * (1.0 / 32.0))
    lower = label - 32.0 * upper
    lane = lax.broadcasted_iota(jnp.int32, (ROWS, META), 1)
    meta = jnp.zeros((ROWS, META), F32)
    for place, value in enumerate((first, second, third, upper, lower, offset)):
        meta = jnp.where(lane == place, value, meta)
    out_ref[:, :D] = x
    out_ref[:, D:] = meta.astype(BF16)


def split_meta(meta):
    wide = meta.astype(F32)
    half = wide[:, 0:1] + wide[:, 1:2] + wide[:, 2:3]
    label = (wide[:, 3:4] * 32.0 + wide[:, 4:5]).astype(jnp.int32)
    return half, label, wide[:, 5:6]


def prep_kernel(block_ref, member_ref, half_ref, count_ref):
    rows = block_ref.shape[0]
    meta = block_ref[:, D:]
    lane = lax.broadcasted_iota(jnp.int32, (8, META), 1)
    pick = jnp.where(lane < 3, 1.0, 0.0).astype(BF16)
    half_ref[...] = lax.dot_general(pick, meta, TRANSPOSED, preferred_element_type=F32)
    _, label, _ = split_meta(meta)
    ids = lax.broadcasted_iota(jnp.int32, (rows, CLUSTERS), 1)
    member = jnp.where(label == ids, 1.0, 0.0)
    count_ref[...] = jnp.sum(member, axis=0, keepdims=True)
    member_ref[...] = member.astype(BF16)


def prep(block):
    rows = block.shape[0]
    outs = (
        shape((rows, CLUSTERS), BF16),
        shape((8, rows), F32),
        shape((1, CLUSTERS), F32),
    )
    return call(prep_kernel, outs, (rows * CLUSTERS * 4, rows * 4096), block)


def main_kernel(blocks, rows_ref, *refs):
    block_refs, refs = refs[:blocks], refs[blocks:]
    member_refs, refs = refs[:blocks], refs[blocks:]
    half_refs, refs = refs[:blocks], refs[blocks:]
    count_refs, refs = refs[:blocks], refs[blocks:]
    out_ref, total_ref = refs
    half, label, offset = split_meta(rows_ref[:, D:])
    right = jnp.concatenate([ref[:, :D] for ref in block_refs], axis=0)
    member = jnp.concatenate([ref[...] for ref in member_refs], axis=0)
    half_row = jnp.concatenate([ref[0:1, :] for ref in half_refs], axis=1)
    count = functools.reduce(jnp.add, [ref[...] for ref in count_refs])
    gram = lax.dot_general(rows_ref[:, :D], right, TRANSPOSED, preferred_element_type=F32)
    kernel = jnp.exp2(gram * SCALE - half - half_row) - offset
    sums = jnp.dot(kernel.astype(BF16), member, preferred_element_type=F32)
    ids = lax.broadcasted_iota(jnp.int32, sums.shape, 1)
    own = jnp.where(label == ids, sums + offset * count, 0.0)
    total_ref[...] = jnp.sum(own, axis=0, keepdims=True)
    out_ref[...] = sums.astype(out_ref.dtype)


def main(rows, dtype, blocks, members, halves, counts):
    outs = (shape((rows.shape[0], CLUSTERS), dtype), shape((1, CLUSTERS), F32))
    flops = 4 * rows.shape[0] * 1280 * 1024
    size = sum(a.size * 2 for a in (rows, *blocks, *members))
    return call(
        functools.partial(main_kernel, len(blocks)),
        outs, (flops, size), rows, *blocks, *members, *halves, *counts,
    )


def sums_kernel(totals, *refs):
    out_ref = refs[-1]
    total = functools.reduce(jnp.add, [ref[...] for ref in refs[:totals]])
    count = functools.reduce(jnp.add, [ref[...] for ref in refs[totals:-1]])
    out_ref[0:1, :] = total
    out_ref[1:2, :] = count * (1.0 / 16.0)


def final_kernel(own_ref, packed_ref, sums_ref, *refs):
    out_ref = refs[-1]
    similar = own_ref[...]
    for ref in refs[:-1]:
        similar = similar + ref[...].astype(F32)
    _, _, offset = split_meta(packed_ref[:, D:])
    totals = sums_ref[0:1, :]
    counts = sums_ref[1:2, :]
    sizes = jnp.maximum(counts, 1.0)
    inverse = 1.0 / sizes
    similar = similar + offset * counts
    out_ref[...] = 1.0 - 2.0 * (similar * inverse) + totals * inverse * inverse


def merge_kernel(own_ref, first_ref, second_ref, third_ref, own_out, *outs):
    sums = own_ref[...]
    for ref in (first_ref, second_ref, third_ref):
        sums = sums + ref[...].astype(F32)
    own_out[...] = sums[:ROWS]
    for place, ref in enumerate(outs):
        ref[...] = sums[(place + 1) * ROWS : (place + 2) * ROWS].astype(BF16)


def gate_kernel(*refs):
    del refs


def gate(value, *after):
    return pl.pallas_call(
        gate_kernel,
        out_shape=shape(value.shape, value.dtype),
        in_specs=[pl.BlockSpec(memory_space=pl.ANY)] * (1 + len(after)),
        out_specs=pl.BlockSpec(memory_space=pl.ANY),
        input_output_aliases={0: 0},
    )(value, *after)


def local(clips, labels):
    def shift(value, axis, step, flip=False):
        names = axis if isinstance(axis, tuple) else (axis,)
        size = 1
        for name in names:
            size *= SIZES[AXES.index(name)]
        pairs = [(i, i ^ step if flip else (i + step) % size) for i in range(size)]
        return lax.ppermute(value, axis, pairs)

    def plane_shift(value, stage, step):
        pairs = []
        for y in range(4):
            for core in range(2):
                for x in range(4):
                    if (core == 0) == (stage == 1):
                        to_y, to_x = y, (x + step) % 4
                    else:
                        to_y, to_x = (y + step) % 4, x
                    pairs.append(((y * 2 + core) * 4 + x, (to_y * 2 + core) * 4 + to_x))
        return lax.ppermute(value, PLANE, pairs)

    def far_shift(value):
        pairs = []
        for core in range(2):
            for z in range(8):
                to_z = (z + (2 if core == 0 else -2)) % 8
                pairs.append((z // 2 * 4 + core * 2 + z % 2, to_z // 2 * 4 + core * 2 + to_z % 2))
        return lax.ppermute(value, ("z_hi", "core", "z_lo"), pairs)

    own = call(
        pack_kernel, shape((ROWS, WIDE), BF16), (10**6, ROWS * WIDE * 4),
        clips, labels.reshape(1, ROWS),
    )
    steps = (1, -1, 2)
    near = [plane_shift(own, 1, step) for step in steps]
    up = [own, shift(own, Z, 1), shift(own, Z, 2)]
    down = [own, shift(own, Z, -1), shift(own, Z, -2)]
    up.append(shift(up[2], Z, 1))
    down.append(shift(down[2], Z, -1))
    up.append(far_shift(jnp.where(lax.axis_index("core") == 0, up[2], down[2])))
    four = jnp.concatenate([own, *near], axis=0)
    rows = [plane_shift(four, 2, step) for step in steps]

    blocks = [
        jnp.concatenate([own, up[1], down[1], up[2]], axis=0),
        jnp.concatenate([down[2], up[3], down[3], up[4]], axis=0),
    ]
    blocks[1] = gate(blocks[1], *rows)
    blocks += [shift(block, "core", 1) for block in blocks]
    members, halves, counts = zip(*[prep(block) for block in blocks])

    received, totals = [], []
    for step, block in zip(steps, rows):
        sums, total = main(block, BF16, blocks, members, halves, counts)
        received.append(plane_shift(sums, 2, -step))
        totals.append(total)
    similar, total = main(four, F32, blocks, members, halves, counts)
    totals.append(total)

    sums = call(
        functools.partial(sums_kernel, 4), shape((2, CLUSTERS), F32), (10**5, 10**5),
        *totals, *counts,
    )
    sums = gate(sums, received[0], received[1])
    for step in (1, 2, 4):
        sums = sums + shift(sums, Z, step, flip=True)
    sums = sums + shift(sums, "core", 1)
    for axis in ("x", "y"):
        parts = [shift(sums, axis, step) for step in (1, 2, 3)]
        sums = sums + parts[0] + parts[1] + parts[2]

    similar, *parts = call(
        merge_kernel,
        (shape((ROWS, CLUSTERS), F32),) + (shape((ROWS, CLUSTERS), BF16),) * 3,
        (10**6, 4 * 10**6), similar, *received,
    )
    parts = [plane_shift(part, 1, -step) for step, part in zip(steps, parts)]
    return call(
        final_kernel, shape((ROWS, CLUSTERS), F32), (10**6, 2 * 10**6),
        similar, own, sums, *parts,
    )


def solution(mesh):
    fine = Mesh(mesh.devices.reshape(SIZES), AXES)
    return jax.shard_map(
        local, mesh=fine, in_specs=(P(AXES, None), P(AXES)), out_specs=P(AXES, None), check_vma=False
    )
```

```python
import functools

import jax
import jax.numpy as jnp
from jax import lax
from jax.experimental import pallas as pl
from jax.experimental.pallas import tpu as pltpu
from jax.sharding import Mesh, PartitionSpec as P

D = 1024
CLUSTERS = 1024
META = 128
WIDE = D + META
ROWS = 80
LOG2E = 1.4426950408889634
SCALE = LOG2E / D
F32 = jnp.float32
SMALL = 8 * 2**20
LARGE = 24 * 2**20
LONG = 3 * 10**9
BF16 = jnp.bfloat16
TRANSPOSED = (((1,), (1,)), ((), ()))
AXES = ("z_hi", "y", "core", "z_lo", "x")
SIZES = (4, 4, 2, 2, 4)
Z = ("z_hi", "z_lo")
PLANE = ("y", "core", "x")


def call(body, outs, cost, *args):
    flops, size = cost
    return pl.pallas_call(
        body,
        out_shape=outs,
        compiler_params=pltpu.CompilerParams(vmem_limit_bytes=LARGE),
        cost_estimate=pl.CostEstimate(flops=flops, bytes_accessed=size, transcendentals=0),
    )(*args)


def shape(dims, dtype):
    return jax.ShapeDtypeStruct(dims, dtype)


def pack_kernel(clips_hbm, labels_hbm, out_ref, clips_ref, labels_ref, clips_sem, labels_sem):
    clips_copy = pltpu.make_async_copy(clips_hbm, clips_ref, clips_sem)
    labels_copy = pltpu.make_async_copy(labels_hbm, labels_ref, labels_sem)
    clips_copy.start()
    labels_copy.start()
    labels_copy.wait()
    clips_copy.wait()
    x = clips_ref[...]
    wide = x.astype(F32)
    half = jnp.sum(wide * wide, axis=1, keepdims=True) * (0.5 * SCALE)
    row = lax.broadcasted_iota(jnp.int32, (ROWS, ROWS), 0)
    col = lax.broadcasted_iota(jnp.int32, (ROWS, ROWS), 1)
    same = row == col
    label = jnp.sum(jnp.where(same, labels_ref[...].astype(F32), 0.0), axis=1, keepdims=True)
    half_row = jnp.sum(jnp.where(same, half, 0.0), axis=0, keepdims=True)
    gram = lax.dot_general(x, x, TRANSPOSED, preferred_element_type=F32)
    near = jnp.exp2(gram * SCALE - half - half_row)
    offset = jnp.sum(jnp.where(same, 0.0, near), axis=1, keepdims=True) * (1.0 / (ROWS - 1))
    first = half.astype(BF16).astype(F32)
    second = (half - first).astype(BF16).astype(F32)
    third = half - first - second
    upper = jnp.floor(label * (1.0 / 32.0))
    lower = label - 32.0 * upper
    lane = lax.broadcasted_iota(jnp.int32, (ROWS, META), 1)
    meta = jnp.zeros((ROWS, META), F32)
    for place, value in enumerate((first, second, third, upper, lower, offset)):
        meta = jnp.where(lane == place, value, meta)
    out_ref[:, :D] = x
    out_ref[:, D:] = meta.astype(BF16)


def split_meta(meta):
    wide = meta.astype(F32)
    half = wide[:, 0:1] + wide[:, 1:2] + wide[:, 2:3]
    label = (wide[:, 3:4] * 32.0 + wide[:, 4:5]).astype(jnp.int32)
    return half, label, wide[:, 5:6]


def prep_kernel(block_ref, member_ref, row_ref, count_ref):
    rows = block_ref.shape[0]
    meta = block_ref[:, D:]
    line = lax.broadcasted_iota(jnp.int32, (8, META), 0)
    lane = lax.broadcasted_iota(jnp.int32, (8, META), 1)
    pick = jnp.where((line == 0) & (lane < 3), 1.0, 0.0)
    pick = jnp.where((line == 1) & (lane == 3), 32.0, pick)
    pick = jnp.where((line == 1) & (lane == 4), 1.0, pick).astype(BF16)
    row_ref[...] = lax.dot_general(pick, meta, TRANSPOSED, preferred_element_type=F32)
    _, label, _ = split_meta(meta)
    ids = lax.broadcasted_iota(jnp.int32, (rows, CLUSTERS), 1)
    member = jnp.where(label == ids, 1.0, 0.0)
    count_ref[...] = jnp.sum(member, axis=0, keepdims=True)
    member_ref[...] = member.astype(BF16)


def prep(block):
    rows = block.shape[0]
    outs = (
        shape((rows, CLUSTERS), BF16),
        shape((8, rows), F32),
        shape((1, CLUSTERS), F32),
    )
    return call(prep_kernel, outs, (0, 0), block)


def kernel_kernel(parts, blocks, *refs):
    part_refs, refs = refs[:parts], refs[parts:]
    block_refs, refs = refs[:blocks], refs[blocks:]
    row_refs, refs = refs[:blocks], refs[blocks:]
    count_refs, refs = refs[:blocks], refs[blocks:]
    out_refs, sums_ref = refs[:parts], refs[parts]
    right = jnp.concatenate([ref[:, :D] for ref in block_refs], axis=0)
    half_row = jnp.concatenate([ref[0:1, :] for ref in row_refs], axis=1)
    label_row = jnp.concatenate([ref[1:2, :] for ref in row_refs], axis=1).astype(jnp.int32)
    total = None
    for part, out in zip(part_refs, out_refs):
        half, label, offset = split_meta(part[:, D:])
        gram = lax.dot_general(part[:, :D], right, TRANSPOSED, preferred_element_type=F32)
        kernel = jnp.exp2(gram * SCALE - half - half_row)
        own = jnp.sum(jnp.where(label == label_row, kernel, 0.0), axis=1, keepdims=True)
        out[...] = (kernel - offset).astype(BF16)
        ids = lax.broadcasted_iota(jnp.int32, (part.shape[0], CLUSTERS), 1)
        term = jnp.sum(jnp.where(label == ids, own, 0.0), axis=0, keepdims=True)
        total = term if total is None else total + term
    sums_ref[0:1, :] = total
    count = functools.reduce(jnp.add, [ref[...] for ref in count_refs])
    sums_ref[1:2, :] = count * (1.0 / 16.0)


def kernels(parts, blocks, rows, counts):
    width = sum(block.shape[0] for block in blocks)
    outs = tuple(shape((part.shape[0], width), BF16) for part in parts)
    return call(
        functools.partial(kernel_kernel, len(parts), len(blocks)),
        outs + (shape((2, CLUSTERS), F32),), (0, 0), *parts, *blocks, *rows, *counts,
    )


def main_kernel(kernel_ref, *refs):
    out_ref = refs[-1]
    member = jnp.concatenate([ref[...] for ref in refs[:-1]], axis=0)
    sums = jnp.dot(kernel_ref[...], member, preferred_element_type=F32)
    out_ref[...] = sums.astype(out_ref.dtype)


def main(kernel, dtype, members):
    return call(main_kernel, shape((kernel.shape[0], CLUSTERS), dtype), (0, 0), kernel, *members)


def merge_kernel(own_ref, first_ref, second_ref, third_ref, sums_ref, own_out, *outs):
    sums = own_ref[...]
    for ref in (first_ref, second_ref, third_ref):
        sums = sums + ref[...].astype(F32)
    own_out[...] = sums[:ROWS]
    rest = sums_ref[...]
    pieces = []
    for _ in range(3):
        pieces.append(rest.astype(BF16).astype(F32))
        rest = rest - pieces[-1]
    extra = jnp.concatenate(pieces + [jnp.zeros((10, CLUSTERS), F32)], axis=0).astype(BF16)
    for place, ref in enumerate(outs):
        ref[:ROWS, :] = sums[(place + 1) * ROWS : (place + 2) * ROWS].astype(BF16)
        ref[ROWS:, :] = extra


def final_kernel(own_ref, packed_ref, sums_ref, *refs):
    out_ref = refs[-1]
    similar = own_ref[...]
    sums = sums_ref[...]
    for ref in refs[:-1]:
        similar = similar + ref[:ROWS, :].astype(F32)
        extra = ref[ROWS:, :].astype(F32)
        sums = sums + (extra[0:2] + extra[2:4] + extra[4:6])
    _, _, offset = split_meta(packed_ref[:, D:])
    totals = sums[0:1, :]
    counts = sums[1:2, :]
    sizes = jnp.maximum(counts, 1.0)
    inverse = 1.0 / sizes
    similar = similar + offset * counts
    out_ref[...] = 1.0 - 2.0 * (similar * inverse) + totals * inverse * inverse


def plus_kernel(count, *refs):
    refs[-1][...] = functools.reduce(jnp.add, [ref[...] for ref in refs[:count]])


def plus(values, after=(), flops=0):
    return call(
        functools.partial(plus_kernel, len(values)),
        shape(values[0].shape, values[0].dtype), (flops, 0), *values, *after,
    )


def relay_kernel(*refs):
    del refs


def relay(values, after=(), flops=0):
    return pl.pallas_call(
        relay_kernel,
        out_shape=[shape(value.shape, value.dtype) for value in values],
        input_output_aliases={place: place for place in range(len(values))},
        compiler_params=pltpu.CompilerParams(vmem_limit_bytes=SMALL),
        cost_estimate=pl.CostEstimate(flops=flops, bytes_accessed=0, transcendentals=0),
    )(*values, *after)


def join_kernel(count, *refs):
    refs[-1][...] = jnp.concatenate([ref[...] for ref in refs[:count]], axis=0)


def join(values, after=(), flops=0):
    rows = sum(value.shape[0] for value in values)
    return call(
        functools.partial(join_kernel, len(values)),
        shape((rows, values[0].shape[1]), values[0].dtype), (flops, 0), *values, *after,
    )


def local(clips, labels):
    def shift(value, axis, step, flip=False):
        names = axis if isinstance(axis, tuple) else (axis,)
        size = 1
        for name in names:
            size *= SIZES[AXES.index(name)]
        pairs = [(i, i ^ step if flip else (i + step) % size) for i in range(size)]
        return lax.ppermute(value, axis, pairs)

    def plane_shift(value, stage, step):
        pairs = []
        for y in range(4):
            for core in range(2):
                for x in range(4):
                    if (core == 0) == (stage == 1):
                        to_y, to_x = y, (x + step) % 4
                    else:
                        to_y, to_x = (y + step) % 4, x
                    pairs.append(((y * 2 + core) * 4 + x, (to_y * 2 + core) * 4 + to_x))
        return lax.ppermute(value, PLANE, pairs)

    own = pl.pallas_call(
        pack_kernel,
        out_shape=shape((ROWS, WIDE), BF16),
        in_specs=[pl.BlockSpec(memory_space=pl.ANY)] * 2,
        out_specs=pl.BlockSpec(memory_space=pltpu.VMEM),
        scratch_shapes=[
            pltpu.VMEM((ROWS, D), BF16),
            pltpu.VMEM((1, ROWS), jnp.int32),
            pltpu.SemaphoreType.DMA,
            pltpu.SemaphoreType.DMA,
        ],
        compiler_params=pltpu.CompilerParams(vmem_limit_bytes=SMALL),
    )(clips, labels.reshape(1, ROWS))
    steps = (1, -1, 2)
    near = [plane_shift(own, 1, step) for step in steps]
    up = [own, shift(own, Z, 1)]
    down = [own, shift(own, Z, -1)]
    four = join([own, *near], after=[up[1], down[1]], flops=10**9)
    rows = [plane_shift(four, 2, step) for step in steps]
    up.append(shift(up[1], Z, 1))
    down.append(shift(down[1], Z, -1))
    up.append(shift(up[2], Z, 1))
    down.append(shift(down[2], Z, -1))
    up.append(shift(up[3], Z, 1))

    blocks = [join([own, *up[1:4], *down[1:4]])]
    blocks += [shift(block, "core", 1) for block in blocks]
    early = [prep(block) for block in blocks]
    blocks.append(join([up[4]], after=[member for member, _, _ in early]))
    blocks.append(shift(blocks[-1], "core", 1))
    members, lines, counts = zip(*early, *[prep(block) for block in blocks[2:]])

    for _ in range(4):
        rows = relay(rows, flops=3 * 10**9)
    *kernel, sums = kernels([*rows, four], blocks, lines, counts)
    terms = [main(part, BF16, members) for part in kernel[:3]]
    received = [plane_shift(term, 2, -step) for step, term in zip(steps, terms)]
    sums = plus([sums, shift(sums, Z, 1, flip=True)], after=terms[:2], flops=LONG)
    others = [shift(sums, Z, step) for step in (2, -2, 4)]
    sums = plus([sums, *others], after=terms[2:], flops=LONG)
    sums = plus([sums, shift(sums, "core", 1)], after=received[:1], flops=LONG)
    others = [plane_shift(sums, 2, step) for step in steps]
    sums = plus([sums, *others], after=received[1:2], flops=LONG)
    similar = main(kernel[3], F32, members)
    similar, *parts = call(
        merge_kernel,
        (shape((ROWS, CLUSTERS), F32),) + (shape((ROWS + 16, CLUSTERS), BF16),) * 3,
        (0, 0), similar, *received, sums,
    )
    parts = [plane_shift(part, 1, -step) for step, part in zip(steps, parts)]
    return call(
        final_kernel, shape((ROWS, CLUSTERS), F32), (0, 0), similar, own, sums, *parts
    )


def solution(mesh):
    fine = Mesh(mesh.devices.reshape(SIZES), AXES)
    return jax.shard_map(
        local, mesh=fine, in_specs=(P(AXES, None), P(AXES)), out_specs=P(AXES, None), check_vma=False
    )
```

```python
import functools

import jax
import jax.numpy as jnp
from jax import lax
from jax.experimental import pallas as pl
from jax.experimental.pallas import tpu as pltpu
from jax.sharding import Mesh, PartitionSpec as P

D = 1024
CLUSTERS = 1024
META = 128
WIDE = D + META
ROWS = 80
LOG2E = 1.4426950408889634
SCALE = LOG2E / D
F32 = jnp.float32
SMALL = 8 * 2**20
LARGE = 24 * 2**20
LONG = 3 * 10**9
BF16 = jnp.bfloat16
TRANSPOSED = (((1,), (1,)), ((), ()))
AXES = ("z_hi", "y", "core", "z_lo", "x")
SIZES = (4, 4, 2, 2, 4)
Z = ("z_hi", "z_lo")
PLANE = ("y", "core", "x")


def call(body, outs, cost, *args):
    flops, size = cost
    return pl.pallas_call(
        body,
        out_shape=outs,
        compiler_params=pltpu.CompilerParams(vmem_limit_bytes=LARGE),
        cost_estimate=pl.CostEstimate(flops=flops, bytes_accessed=size, transcendentals=0),
    )(*args)


def shape(dims, dtype):
    return jax.ShapeDtypeStruct(dims, dtype)


def pack_kernel(clips_hbm, labels_hbm, out_ref, clips_ref, labels_ref, clips_sem, labels_sem):
    clips_copy = pltpu.make_async_copy(clips_hbm, clips_ref, clips_sem)
    labels_copy = pltpu.make_async_copy(labels_hbm, labels_ref, labels_sem)
    clips_copy.start()
    labels_copy.start()
    labels_copy.wait()
    clips_copy.wait()
    x = clips_ref[...]
    wide = x.astype(F32)
    half = jnp.sum(wide * wide, axis=1, keepdims=True) * (0.5 * SCALE)
    row = lax.broadcasted_iota(jnp.int32, (ROWS, ROWS), 0)
    col = lax.broadcasted_iota(jnp.int32, (ROWS, ROWS), 1)
    same = row == col
    label = jnp.sum(jnp.where(same, labels_ref[...].astype(F32), 0.0), axis=1, keepdims=True)
    half_row = jnp.sum(jnp.where(same, half, 0.0), axis=0, keepdims=True)
    gram = lax.dot_general(x, x, TRANSPOSED, preferred_element_type=F32)
    near = jnp.exp2(gram * SCALE - half - half_row)
    offset = jnp.sum(jnp.where(same, 0.0, near), axis=1, keepdims=True) * (1.0 / (ROWS - 1))
    first = half.astype(BF16).astype(F32)
    second = (half - first).astype(BF16).astype(F32)
    third = half - first - second
    upper = jnp.floor(label * (1.0 / 32.0))
    lower = label - 32.0 * upper
    lane = lax.broadcasted_iota(jnp.int32, (ROWS, META), 1)
    meta = jnp.zeros((ROWS, META), F32)
    for place, value in enumerate((first, second, third, upper, lower, offset)):
        meta = jnp.where(lane == place, value, meta)
    out_ref[:, :D] = x
    out_ref[:, D:] = meta.astype(BF16)


def split_meta(meta):
    wide = meta.astype(F32)
    half = wide[:, 0:1] + wide[:, 1:2] + wide[:, 2:3]
    label = (wide[:, 3:4] * 32.0 + wide[:, 4:5]).astype(jnp.int32)
    return half, label, wide[:, 5:6]


def prep_kernel(block_ref, member_ref, row_ref, count_ref):
    rows = block_ref.shape[0]
    meta = block_ref[:, D:]
    line = lax.broadcasted_iota(jnp.int32, (8, META), 0)
    lane = lax.broadcasted_iota(jnp.int32, (8, META), 1)
    pick = jnp.where((line == 0) & (lane < 3), 1.0, 0.0)
    pick = jnp.where((line == 1) & (lane == 3), 32.0, pick)
    pick = jnp.where((line == 1) & (lane == 4), 1.0, pick).astype(BF16)
    row_ref[...] = lax.dot_general(pick, meta, TRANSPOSED, preferred_element_type=F32)
    _, label, _ = split_meta(meta)
    ids = lax.broadcasted_iota(jnp.int32, (rows, CLUSTERS), 1)
    member = jnp.where(label == ids, 1.0, 0.0)
    count_ref[...] = jnp.sum(member, axis=0, keepdims=True)
    member_ref[...] = member.astype(BF16)


def prep(block):
    rows = block.shape[0]
    outs = (
        shape((rows, CLUSTERS), BF16),
        shape((8, rows), F32),
        shape((1, CLUSTERS), F32),
    )
    return call(prep_kernel, outs, (0, 0), block)


def kernel_kernel(parts, blocks, *refs):
    part_refs, refs = refs[:parts], refs[parts:]
    block_refs, refs = refs[:blocks], refs[blocks:]
    row_refs, refs = refs[:blocks], refs[blocks:]
    count_refs, refs = refs[:blocks], refs[blocks:]
    out_refs, sums_ref = refs[:parts], refs[parts]
    right = jnp.concatenate([ref[:, :D] for ref in block_refs], axis=0)
    half_row = jnp.concatenate([ref[0:1, :] for ref in row_refs], axis=1)
    label_row = jnp.concatenate([ref[1:2, :] for ref in row_refs], axis=1).astype(jnp.int32)
    total = None
    for part, out in zip(part_refs, out_refs):
        half, label, offset = split_meta(part[:, D:])
        gram = lax.dot_general(part[:, :D], right, TRANSPOSED, preferred_element_type=F32)
        kernel = jnp.exp2(gram * SCALE - half - half_row)
        own = jnp.sum(jnp.where(label == label_row, kernel, 0.0), axis=1, keepdims=True)
        out[...] = (kernel - offset).astype(BF16)
        ids = lax.broadcasted_iota(jnp.int32, (part.shape[0], CLUSTERS), 1)
        term = jnp.sum(jnp.where(label == ids, own, 0.0), axis=0, keepdims=True)
        total = term if total is None else total + term
    sums_ref[0:1, :] = total
    count = functools.reduce(jnp.add, [ref[...] for ref in count_refs])
    sums_ref[1:2, :] = count * (1.0 / 16.0)


def kernels(parts, blocks, rows, counts):
    width = sum(block.shape[0] for block in blocks)
    outs = tuple(shape((part.shape[0], width), BF16) for part in parts)
    return call(
        functools.partial(kernel_kernel, len(parts), len(blocks)),
        outs + (shape((2, CLUSTERS), F32),), (0, 0), *parts, *blocks, *rows, *counts,
    )


def main_kernel(kernel_ref, *refs):
    out_ref = refs[-1]
    member = jnp.concatenate([ref[...] for ref in refs[:-1]], axis=0)
    sums = jnp.dot(kernel_ref[...], member, preferred_element_type=F32)
    out_ref[...] = sums.astype(out_ref.dtype)


def main(kernel, dtype, members):
    return call(main_kernel, shape((kernel.shape[0], CLUSTERS), dtype), (0, 0), kernel, *members)


def merge_kernel(own_ref, first_ref, second_ref, third_ref, sums_ref, own_out, *outs):
    sums = own_ref[...]
    for ref in (first_ref, second_ref, third_ref):
        sums = sums + ref[...].astype(F32)
    own_out[...] = sums[:ROWS]
    rest = sums_ref[...]
    pieces = []
    for _ in range(3):
        pieces.append(rest.astype(BF16).astype(F32))
        rest = rest - pieces[-1]
    extra = jnp.concatenate(pieces + [jnp.zeros((10, CLUSTERS), F32)], axis=0).astype(BF16)
    for place, ref in enumerate(outs):
        ref[:ROWS, :] = sums[(place + 1) * ROWS : (place + 2) * ROWS].astype(BF16)
        ref[ROWS:, :] = extra


def final_kernel(own_ref, packed_ref, sums_ref, *refs):
    out_ref = refs[-1]
    similar = own_ref[...]
    sums = sums_ref[...]
    for ref in refs[:-1]:
        similar = similar + ref[:ROWS, :].astype(F32)
        extra = ref[ROWS:, :].astype(F32)
        sums = sums + (extra[0:2] + extra[2:4] + extra[4:6])
    _, _, offset = split_meta(packed_ref[:, D:])
    totals = sums[0:1, :]
    counts = sums[1:2, :]
    sizes = jnp.maximum(counts, 1.0)
    inverse = 1.0 / sizes
    similar = similar + offset * counts
    out_ref[...] = 1.0 - 2.0 * (similar * inverse) + totals * inverse * inverse


def plus_kernel(count, *refs):
    refs[-1][...] = functools.reduce(jnp.add, [ref[...] for ref in refs[:count]])


def plus(values, after=(), flops=0):
    return call(
        functools.partial(plus_kernel, len(values)),
        shape(values[0].shape, values[0].dtype), (flops, 0), *values, *after,
    )


def relay_kernel(*refs):
    del refs


def relay(values, after=(), flops=0):
    return pl.pallas_call(
        relay_kernel,
        out_shape=[shape(value.shape, value.dtype) for value in values],
        input_output_aliases={place: place for place in range(len(values))},
        compiler_params=pltpu.CompilerParams(vmem_limit_bytes=SMALL),
        cost_estimate=pl.CostEstimate(flops=flops, bytes_accessed=0, transcendentals=0),
    )(*values, *after)


def join_kernel(count, *refs):
    refs[-1][...] = jnp.concatenate([ref[...] for ref in refs[:count]], axis=0)


def join(values, after=(), flops=0):
    rows = sum(value.shape[0] for value in values)
    return call(
        functools.partial(join_kernel, len(values)),
        shape((rows, values[0].shape[1]), values[0].dtype), (flops, 0), *values, *after,
    )


def local(clips, labels):
    def shift(value, axis, step, flip=False):
        names = axis if isinstance(axis, tuple) else (axis,)
        size = 1
        for name in names:
            size *= SIZES[AXES.index(name)]
        pairs = [(i, i ^ step if flip else (i + step) % size) for i in range(size)]
        return lax.ppermute(value, axis, pairs)

    def plane_shift(value, stage, step):
        pairs = []
        for y in range(4):
            for core in range(2):
                for x in range(4):
                    if (core == 0) == (stage == 1):
                        to_y, to_x = y, (x + step) % 4
                    else:
                        to_y, to_x = (y + step) % 4, x
                    pairs.append(((y * 2 + core) * 4 + x, (to_y * 2 + core) * 4 + to_x))
        return lax.ppermute(value, PLANE, pairs)

    own = pl.pallas_call(
        pack_kernel,
        out_shape=shape((ROWS, WIDE), BF16),
        in_specs=[pl.BlockSpec(memory_space=pl.ANY)] * 2,
        out_specs=pl.BlockSpec(memory_space=pltpu.VMEM),
        scratch_shapes=[
            pltpu.VMEM((ROWS, D), BF16),
            pltpu.VMEM((1, ROWS), jnp.int32),
            pltpu.SemaphoreType.DMA,
            pltpu.SemaphoreType.DMA,
        ],
        compiler_params=pltpu.CompilerParams(vmem_limit_bytes=SMALL),
    )(clips, labels.reshape(1, ROWS))
    steps = (1, -1, 2)
    near = [plane_shift(own, 1, step) for step in steps]
    up = [own, shift(own, Z, 1)]
    down = [own, shift(own, Z, -1)]
    four = join([own, *near], after=[up[1], down[1]], flops=10**9)
    rows = [plane_shift(four, 2, step) for step in steps]
    up.append(shift(up[1], Z, 1))
    down.append(shift(down[1], Z, -1))
    up.append(shift(up[2], Z, 1))
    down.append(shift(down[2], Z, -1))
    up.append(shift(down[3], Z, -1))

    blocks = [join([own, *up[1:4], *down[1:4]])]
    blocks += [shift(block, "core", 1) for block in blocks]
    early = [prep(block) for block in blocks]
    blocks.append(join([up[4]], after=[member for member, _, _ in early], flops=0))
    blocks.append(shift(blocks[-1], "core", 1))
    members, lines, counts = zip(*early, *[prep(block) for block in blocks[2:]])

    for _ in range(4):
        rows = relay(rows, flops=3 * 10**9)
    *kernel, sums = kernels([*rows, four], blocks, lines, counts)
    terms = [main(part, BF16, members) for part in kernel[:3]]
    received = [plane_shift(term, 2, -step) for step, term in zip(steps, terms)]
    below, above = shift(sums, Z, 1), shift(sums, Z, -1)
    two = plus([sums, below], flops=0)
    sums = plus([sums, below, above], after=terms[:2], flops=LONG)
    sums = plus([sums, shift(sums, Z, 3), shift(two, Z, -3)], after=terms[2:], flops=LONG)
    sums = plus([sums, shift(sums, "core", 1)], after=received[:1], flops=LONG)
    others = [plane_shift(sums, 2, step) for step in steps]
    sums = plus([sums, *others], after=received[1:2], flops=LONG)
    similar = main(kernel[3], F32, members)
    similar, *parts = call(
        merge_kernel,
        (shape((ROWS, CLUSTERS), F32),) + (shape((ROWS + 16, CLUSTERS), BF16),) * 3,
        (0, 0), similar, *received, sums,
    )
    parts = [plane_shift(part, 1, -step) for step, part in zip(steps, parts)]
    return call(
        final_kernel, shape((ROWS, CLUSTERS), F32), (0, 0), similar, own, sums, *parts
    )


def solution(mesh):
    fine = Mesh(mesh.devices.reshape(SIZES), AXES)
    return jax.shard_map(
        local, mesh=fine, in_specs=(P(AXES, None), P(AXES)), out_specs=P(AXES, None), check_vma=False
    )
```

```python
import functools

import jax
import jax.numpy as jnp
from jax import lax
from jax.experimental import pallas as pl
from jax.experimental.pallas import tpu as pltpu
from jax.sharding import Mesh, PartitionSpec as P

D = 1024
CLUSTERS = 1024
META = 128
WIDE = D + META
ROWS = 80
LOG2E = 1.4426950408889634
SCALE = LOG2E / D
F32 = jnp.float32
SMALL = 8 * 2**20
LARGE = 24 * 2**20
LONG = 3 * 10**9
BF16 = jnp.bfloat16
TRANSPOSED = (((1,), (1,)), ((), ()))
AXES = ("z_hi", "y", "core", "z_lo", "x")
SIZES = (4, 4, 2, 2, 4)
Z = ("z_hi", "z_lo")
PLANE = ("y", "core", "x")


def call(body, outs, cost, *args):
    flops, size = cost
    return pl.pallas_call(
        body,
        out_shape=outs,
        compiler_params=pltpu.CompilerParams(vmem_limit_bytes=LARGE),
        cost_estimate=pl.CostEstimate(flops=flops, bytes_accessed=size, transcendentals=0),
    )(*args)


def shape(dims, dtype):
    return jax.ShapeDtypeStruct(dims, dtype)


def pack_kernel(clips_hbm, labels_hbm, out_ref, clips_ref, labels_ref, clips_sem, labels_sem):
    clips_copy = pltpu.make_async_copy(clips_hbm, clips_ref, clips_sem)
    labels_copy = pltpu.make_async_copy(labels_hbm, labels_ref, labels_sem)
    clips_copy.start()
    labels_copy.start()
    labels_copy.wait()
    clips_copy.wait()
    x = clips_ref[...]
    wide = x.astype(F32)
    half = jnp.sum(wide * wide, axis=1, keepdims=True) * (0.5 * SCALE)
    row = lax.broadcasted_iota(jnp.int32, (ROWS, ROWS), 0)
    col = lax.broadcasted_iota(jnp.int32, (ROWS, ROWS), 1)
    same = row == col
    label = jnp.sum(jnp.where(same, labels_ref[...].astype(F32), 0.0), axis=1, keepdims=True)
    half_row = jnp.sum(jnp.where(same, half, 0.0), axis=0, keepdims=True)
    gram = lax.dot_general(x, x, TRANSPOSED, preferred_element_type=F32)
    near = jnp.exp2(gram * SCALE - half - half_row)
    offset = jnp.sum(jnp.where(same, 0.0, near), axis=1, keepdims=True) * (1.0 / (ROWS - 1))
    first = half.astype(BF16).astype(F32)
    second = (half - first).astype(BF16).astype(F32)
    third = half - first - second
    upper = jnp.floor(label * (1.0 / 32.0))
    lower = label - 32.0 * upper
    lane = lax.broadcasted_iota(jnp.int32, (ROWS, META), 1)
    meta = jnp.zeros((ROWS, META), F32)
    for place, value in enumerate((first, second, third, upper, lower, offset)):
        meta = jnp.where(lane == place, value, meta)
    out_ref[:, :D] = x
    out_ref[:, D:] = meta.astype(BF16)


def split_meta(meta):
    wide = meta.astype(F32)
    half = wide[:, 0:1] + wide[:, 1:2] + wide[:, 2:3]
    label = (wide[:, 3:4] * 32.0 + wide[:, 4:5]).astype(jnp.int32)
    return half, label, wide[:, 5:6]


def prep_kernel(block_ref, member_ref, row_ref, count_ref):
    rows = block_ref.shape[0]
    meta = block_ref[:, D:]
    line = lax.broadcasted_iota(jnp.int32, (8, META), 0)
    lane = lax.broadcasted_iota(jnp.int32, (8, META), 1)
    pick = jnp.where((line == 0) & (lane < 3), 1.0, 0.0)
    pick = jnp.where((line == 1) & (lane == 3), 32.0, pick)
    pick = jnp.where((line == 1) & (lane == 4), 1.0, pick).astype(BF16)
    row_ref[...] = lax.dot_general(pick, meta, TRANSPOSED, preferred_element_type=F32)
    _, label, _ = split_meta(meta)
    ids = lax.broadcasted_iota(jnp.int32, (rows, CLUSTERS), 1)
    member = jnp.where(label == ids, 1.0, 0.0)
    count_ref[...] = jnp.sum(member, axis=0, keepdims=True)
    member_ref[...] = member.astype(BF16)


def prep(block):
    rows = block.shape[0]
    outs = (
        shape((rows, CLUSTERS), BF16),
        shape((8, rows), F32),
        shape((1, CLUSTERS), F32),
    )
    return call(prep_kernel, outs, (0, 0), block)


def kernel_kernel(parts, blocks, *refs):
    part_refs, refs = refs[:parts], refs[parts:]
    block_refs, refs = refs[:blocks], refs[blocks:]
    row_refs, refs = refs[:blocks], refs[blocks:]
    count_refs, refs = refs[:blocks], refs[blocks:]
    out_refs, sums_ref = refs[:parts], refs[parts]
    right = jnp.concatenate([ref[:, :D] for ref in block_refs], axis=0)
    half_row = jnp.concatenate([ref[0:1, :] for ref in row_refs], axis=1)
    label_row = jnp.concatenate([ref[1:2, :] for ref in row_refs], axis=1).astype(jnp.int32)
    total = None
    for part, out in zip(part_refs, out_refs):
        half, label, offset = split_meta(part[:, D:])
        gram = lax.dot_general(part[:, :D], right, TRANSPOSED, preferred_element_type=F32)
        kernel = jnp.exp2(gram * SCALE - half - half_row)
        own = jnp.sum(jnp.where(label == label_row, kernel, 0.0), axis=1, keepdims=True)
        out[...] = (kernel - offset).astype(BF16)
        ids = lax.broadcasted_iota(jnp.int32, (part.shape[0], CLUSTERS), 1)
        term = jnp.sum(jnp.where(label == ids, own, 0.0), axis=0, keepdims=True)
        total = term if total is None else total + term
    sums_ref[0:1, :] = total
    count = functools.reduce(jnp.add, [ref[...] for ref in count_refs])
    sums_ref[1:2, :] = count * (1.0 / 16.0)


def kernels(parts, blocks, rows, counts):
    width = sum(block.shape[0] for block in blocks)
    outs = tuple(shape((part.shape[0], width), BF16) for part in parts)
    return call(
        functools.partial(kernel_kernel, len(parts), len(blocks)),
        outs + (shape((2, CLUSTERS), F32),), (0, 0), *parts, *blocks, *rows, *counts,
    )


def main_kernel(kernel_ref, *refs):
    out_ref = refs[-1]
    member = jnp.concatenate([ref[...] for ref in refs[:-1]], axis=0)
    sums = jnp.dot(kernel_ref[...], member, preferred_element_type=F32)
    out_ref[...] = sums.astype(out_ref.dtype)


def main(kernel, dtype, members):
    return call(main_kernel, shape((kernel.shape[0], CLUSTERS), dtype), (0, 0), kernel, *members)


def merge_kernel(own_ref, first_ref, second_ref, third_ref, sums_ref, own_out, *outs):
    sums = own_ref[...]
    for ref in (first_ref, second_ref, third_ref):
        sums = sums + ref[...].astype(F32)
    own_out[...] = sums[:ROWS]
    rest = sums_ref[...]
    pieces = []
    for _ in range(3):
        pieces.append(rest.astype(BF16).astype(F32))
        rest = rest - pieces[-1]
    extra = jnp.concatenate(pieces + [jnp.zeros((10, CLUSTERS), F32)], axis=0).astype(BF16)
    for place, ref in enumerate(outs):
        ref[:ROWS, :] = sums[(place + 1) * ROWS : (place + 2) * ROWS].astype(BF16)
        ref[ROWS:, :] = extra


def final_kernel(own_ref, packed_ref, sums_ref, *refs):
    out_ref = refs[-1]
    similar = own_ref[...]
    sums = sums_ref[...]
    for ref in refs[:-1]:
        similar = similar + ref[:ROWS, :].astype(F32)
        extra = ref[ROWS:, :].astype(F32)
        sums = sums + (extra[0:2] + extra[2:4] + extra[4:6])
    _, _, offset = split_meta(packed_ref[:, D:])
    totals = sums[0:1, :]
    counts = sums[1:2, :]
    sizes = jnp.maximum(counts, 1.0)
    inverse = 1.0 / sizes
    similar = similar + offset * counts
    out_ref[...] = 1.0 - 2.0 * (similar * inverse) + totals * inverse * inverse


def plus_kernel(count, *refs):
    refs[-1][...] = functools.reduce(jnp.add, [ref[...] for ref in refs[:count]])


def plus(values, after=(), flops=0):
    return call(
        functools.partial(plus_kernel, len(values)),
        shape(values[0].shape, values[0].dtype), (flops, 0), *values, *after,
    )


def relay_kernel(*refs):
    del refs


def relay(values, after=(), flops=0):
    return pl.pallas_call(
        relay_kernel,
        out_shape=[shape(value.shape, value.dtype) for value in values],
        input_output_aliases={place: place for place in range(len(values))},
        compiler_params=pltpu.CompilerParams(vmem_limit_bytes=SMALL),
        cost_estimate=pl.CostEstimate(flops=flops, bytes_accessed=0, transcendentals=0),
    )(*values, *after)


def join_kernel(count, *refs):
    refs[-1][...] = jnp.concatenate([ref[...] for ref in refs[:count]], axis=0)


def join(values, after=(), flops=0):
    rows = sum(value.shape[0] for value in values)
    return call(
        functools.partial(join_kernel, len(values)),
        shape((rows, values[0].shape[1]), values[0].dtype), (flops, 0), *values, *after,
    )


def local(clips, labels):
    def shift(value, axis, step, flip=False):
        names = axis if isinstance(axis, tuple) else (axis,)
        size = 1
        for name in names:
            size *= SIZES[AXES.index(name)]
        pairs = [(i, i ^ step if flip else (i + step) % size) for i in range(size)]
        return lax.ppermute(value, axis, pairs)

    def plane_shift(value, stage, step):
        pairs = []
        for y in range(4):
            for core in range(2):
                for x in range(4):
                    if (core == 0) == (stage == 1):
                        to_y, to_x = y, (x + step) % 4
                    else:
                        to_y, to_x = (y + step) % 4, x
                    pairs.append(((y * 2 + core) * 4 + x, (to_y * 2 + core) * 4 + to_x))
        return lax.ppermute(value, PLANE, pairs)

    def cross_shift(value):
        pairs = []
        for core in range(2):
            for z in range(8):
                to_z, to_core = (z + 1) % 8, 1 - core
                pairs.append((z // 2 * 4 + core * 2 + z % 2, to_z // 2 * 4 + to_core * 2 + to_z % 2))
        return lax.ppermute(value, ("z_hi", "core", "z_lo"), pairs)

    own = pl.pallas_call(
        pack_kernel,
        out_shape=shape((ROWS, WIDE), BF16),
        in_specs=[pl.BlockSpec(memory_space=pl.ANY)] * 2,
        out_specs=pl.BlockSpec(memory_space=pltpu.VMEM),
        scratch_shapes=[
            pltpu.VMEM((ROWS, D), BF16),
            pltpu.VMEM((1, ROWS), jnp.int32),
            pltpu.SemaphoreType.DMA,
            pltpu.SemaphoreType.DMA,
        ],
        compiler_params=pltpu.CompilerParams(vmem_limit_bytes=SMALL),
    )(clips, labels.reshape(1, ROWS))
    steps = (1, -1, 2)
    near = [plane_shift(own, 1, step) for step in steps]
    up = [own, shift(own, Z, 1)]
    down = [own, shift(own, Z, -1)]
    four = join([own, *near], after=[up[1], down[1]], flops=10**9)
    rows = [plane_shift(four, 2, step) for step in steps]
    up.append(shift(up[1], Z, 1))
    down.append(shift(down[1], Z, -1))
    up.append(shift(up[2], Z, 1))
    down.append(shift(down[2], Z, -1))
    up.append(shift(down[3], Z, -1))

    cross = cross_shift(up[3])
    blocks = [join([own, *up[1:4], *down[1:4]])]
    blocks += [shift(block, "core", 1) for block in blocks]
    early = [prep(block) for block in blocks]
    blocks += [up[4], cross]
    members, lines, counts = zip(*early, *[prep(block) for block in blocks[2:]])

    for _ in range(3):
        rows = relay(rows, flops=3 * 10**9)
    *kernel, sums = kernels([*rows, four], blocks, lines, counts)
    terms = [main(part, BF16, members) for part in kernel[:3]]
    received = [plane_shift(term, 2, -step) for step, term in zip(steps, terms)]
    below, above = shift(sums, Z, 1), shift(sums, Z, -1)
    two = plus([sums, below], flops=0)
    sums = plus([sums, below, above], after=terms[:2], flops=LONG)
    sums = plus([sums, shift(sums, Z, 3), shift(two, Z, -3)], after=terms[2:], flops=LONG)
    sums = plus([sums, shift(sums, "core", 1)], after=received[:1], flops=LONG)
    others = [plane_shift(sums, 2, step) for step in steps]
    sums = plus([sums, *others], after=received[1:2], flops=LONG)
    similar = main(kernel[3], F32, members)
    similar, *parts = call(
        merge_kernel,
        (shape((ROWS, CLUSTERS), F32),) + (shape((ROWS + 16, CLUSTERS), BF16),) * 3,
        (0, 0), similar, *received, sums,
    )
    parts = [plane_shift(part, 1, -step) for step, part in zip(steps, parts)]
    return call(
        final_kernel, shape((ROWS, CLUSTERS), F32), (0, 0), similar, own, sums, *parts
    )


def solution(mesh):
    fine = Mesh(mesh.devices.reshape(SIZES), AXES)
    return jax.shard_map(
        local, mesh=fine, in_specs=(P(AXES, None), P(AXES)), out_specs=P(AXES, None), check_vma=False
    )
```
